32 devices in a mesh: dp: 8 (over z, x), zero: 4 (over y, core).
Axes of the slice: x: 2, y: 2, z: 4, core: 2. Of those that a mesh axis runs over, the one named last changes fastest.
Arguments:
- tokens: bfloat16 [64, 512, 768], P(('dp', 'zero')), may hold values from -6 to 6
- cotangent: bfloat16 [64, 512, 768], P(('dp', 'zero')), may hold values from -6 to 6
- lengths: int32 [64], P(('dp', 'zero')), may hold values from 128 to 512, as said below
- w_qkv: float32 [768, 2304], P('zero'), may hold values from -0.21875 to 0.21875
- w_out: float32 [768, 768], P('zero'), may hold values from -2.5 to 2.5
- w_up: float32 [768, 3072], P('zero'), may hold values from -0.21875 to 0.21875
- w_down: float32 [3072, 768], P('zero'), may hold values from -0.109375 to 0.109375
- vectors: float32 [12, 768], P(None, 'zero'), as said below
- first_qkv: float32 [768, 2304], P('zero')
- first_out: float32 [768, 768], P('zero')
- first_up: float32 [768, 3072], P('zero')
- first_down: float32 [3072, 768], P('zero')
- first_vectors: float32 [12, 768], P(None, 'zero')
- second_qkv: float32 [768, 2304], P('zero'), as said below
- second_out: float32 [768, 768], P('zero'), as said below
- second_up: float32 [768, 3072], P('zero'), as said below
- second_down: float32 [3072, 768], P('zero'), as said below
- second_vectors: float32 [12, 768], P(None, 'zero'), as said below
Outputs:
- output: float32 [64, 512, 768], P(('dp', 'zero'))
- input_grad: float32 [64, 512, 768], P(('dp', 'zero'))
- grad_qkv: float32 [768, 2304], P('zero')
- grad_out: float32 [768, 768], P('zero')
- grad_up: float32 [768, 3072], P('zero')
- grad_down: float32 [3072, 768], P('zero')
- grad_vectors: float32 [12, 768], P(None, 'zero')
- new_qkv: float32 [768, 2304], P('zero')
- new_out: float32 [768, 768], P('zero')
- new_up: float32 [768, 3072], P('zero')
- new_down: float32 [3072, 768], P('zero')
- new_vectors: float32 [12, 768], P(None, 'zero')
- first_qkv_new: float32 [768, 2304], P('zero')
- first_out_new: float32 [768, 768], P('zero')
- first_up_new: float32 [768, 3072], P('zero')
- first_down_new: float32 [3072, 768], P('zero')
- first_vectors_new: float32 [12, 768], P(None, 'zero')
- second_qkv_new: float32 [768, 2304], P('zero')
- second_out_new: float32 [768, 768], P('zero')
- second_up_new: float32 [768, 3072], P('zero')
- second_down_new: float32 [3072, 768], P('zero')
- second_vectors_new: float32 [12, 768], P(None, 'zero')
The draws below stay inside these ranges and needn't reach their ends.
Inputs may be any that keep to these rules, and one draw needn't show every extreme that they name: `lengths`: positions at or past a slot's length are padding; some slot has length exactly 512, and some other slot exactly 128. `vectors`: no biases or gains outside a few units. `second_qkv`: strictly positive. `second_out`: strictly positive. `second_up`: strictly positive. `second_down`: strictly positive. `second_vectors`: strictly positive.
All inputs are finite; a program needn't handle non-finite values.
Results may differ from the reference program's by a relative error of at most 0.013.
The reference program's roundings to bfloat16 on the way count: a program that leaves them out, or rounds other values in their place, can miss the bound.
Values may be sent and summed in bfloat16 or wider, within the bound.
No kernel may reach another device: no remote copies, remote signals or barrier semaphores. Data moves between devices by JAX's collectives and lax.ppermute only.
A program may use at most 256 MiB of HBM per device.

```python
import math
import jax
import jax.numpy as jnp
from jax import lax

D = 768
HEADS = 12
HEAD_DIM = 64
FF = 3072
L = 512
STEP = 10
SEQS = 64
N_DP = 8


def counted_scale(factor):
    return factor * math.sqrt(SEQS * L * 5 / 8)


def log_spread(key, shape, lower, upper):
    return jnp.exp(jax.random.uniform(key, shape, jnp.float32, math.log(lower), math.log(upper)))


def first_moment(key, shape, factor):
    key_size, key_sign = jax.random.split(key)
    magnitude = log_spread(key_size, shape, 0.5, 2.0)
    sign_flip = jnp.where(jax.random.uniform(key_sign, shape, jnp.float32) < 0.5, -1.0, 1.0)
    return (factor * (0.1 / 0.9) * magnitude * sign_flip).astype(jnp.float32)


def second_moment(key, shape, factor):
    return (factor * factor * (0.001 / 0.999) * log_spread(key, shape, 0.5, 6.0)).astype(jnp.float32)


def vector_factor():
    row_scale = jnp.array([0.7, 0.7, 0.7, 0.8, 0.95, 0.95, 1.0, 1.0, 0.25, 0.25, 0.25, 0.25], jnp.float32)
    return row_scale[:, None] * counted_scale(1.0)


def draw_lengths(key, part):
    key = jax.random.fold_in(key, 5)
    key_len, key_pos, key_gap = jax.random.split(key, 3)
    drawn = jax.random.randint(key_len, (SEQS,), L // 4, L + 1, jnp.int32)
    chosen = jax.random.randint(key_pos, (), 0, SEQS, jnp.int32)
    gap = jax.random.randint(key_gap, (), 1, SEQS, jnp.int32)
    shortest = (chosen + gap) % SEQS
    slots = jnp.arange(SEQS, dtype=jnp.int32)
    drawn = jnp.where(slots == shortest, L // 4, drawn)
    return jnp.where(slots == chosen, L, drawn).astype(jnp.int32)


def draw_vectors(key, part):
    key = jax.random.fold_in(key, 3)
    key_bias, key_gain = jax.random.split(key)
    biases = jnp.clip(0.2 * jax.random.normal(key_bias, (12, D), jnp.float32), -0.8, 0.8)
    gains = jax.random.uniform(key_gain, (12, D), jnp.float32, 0.6, 1.6)
    row_index = jnp.arange(12)[:, None]
    return jnp.where((row_index == 4) | (row_index == 6), gains, biases).astype(jnp.float32)


def draw_first_qkv(key, part):
    key = jax.random.fold_in(key, 21)
    return first_moment(key, (D, 3 * D), counted_scale(0.7))


def draw_first_out(key, part):
    key = jax.random.fold_in(key, 22)
    return first_moment(key, (D, D), counted_scale(0.7 * math.sqrt(4.5 / L)))


def draw_first_up(key, part):
    key = jax.random.fold_in(key, 23)
    return first_moment(key, (D, FF), counted_scale(0.25))


def draw_first_down(key, part):
    key = jax.random.fold_in(key, 24)
    return first_moment(key, (FF, D), counted_scale(0.5))


def draw_first_vectors(key, part):
    key = jax.random.fold_in(key, 25)
    return first_moment(key, (12, D), vector_factor())


def draw_second_qkv(key, part):
    key = jax.random.fold_in(key, 31)
    return second_moment(key, (D, 3 * D), counted_scale(0.7))


def draw_second_out(key, part):
    key = jax.random.fold_in(key, 32)
    return second_moment(key, (D, D), counted_scale(0.7 * math.sqrt(4.5 / L)))


def draw_second_up(key, part):
    key = jax.random.fold_in(key, 33)
    return second_moment(key, (D, FF), counted_scale(0.25))


def draw_second_down(key, part):
    key = jax.random.fold_in(key, 34)
    return second_moment(key, (FF, D), counted_scale(0.5))


def draw_second_vectors(key, part):
    key = jax.random.fold_in(key, 35)
    return second_moment(key, (12, D), vector_factor())


def raised(entries, rng, source, target, blocks, factor):
    owner, partner = [(jnp.arange(entries.shape[dim]) // (entries.shape[dim] // blocks)).reshape([-1 if axis == dim else 1 for axis in range(entries.ndim)]) for dim in (source, target)]
    chosen = jax.random.permutation(rng, blocks)[partner]
    strong = (owner == chosen) | (owner == (partner + blocks // 2) % blocks)
    return jnp.where(strong, factor * entries, entries)


def block_scale(key, dims, cuts, smallest, top_value):
    def one(axis_at, blocks):
        heights = jax.random.uniform(jax.random.fold_in(jax.random.fold_in(key, 6), axis_at), (blocks,), jnp.float32, smallest / len(cuts), top_value / len(cuts))
        return jnp.repeat(jnp.exp(heights), dims[axis_at] // blocks).reshape((-1,) + (1,) * (len(dims) - axis_at - 1))

    level = one(*cuts[0])
    for cut in cuts[1:]:
        level = level * one(*cut)
    return level


def gaussian(own_key, extent, spread, bound, cuts=(), kind=jnp.bfloat16):
    loudness = block_scale(own_key, extent, cuts, -0.22, 0.18) if cuts else 1.0
    values = jax.random.normal(own_key, extent, jnp.float32) * spread * loudness
    return jnp.minimum(jnp.maximum(values, -bound), bound).astype(kind)


def gaussian_with(key, shape, spread, limit, cuts, heavy, kind=jnp.bfloat16):
    entries = spread * jax.random.normal(key, shape, jnp.float32)
    if cuts:
        entries = entries * block_scale(key, shape, cuts, -0.22, 0.18)
    return jnp.clip(raised(entries, jax.random.fold_in(key, 3), *heavy), -limit, limit).astype(kind)


def setup_inputs(seed: int = 0) -> dict:
    splits = jax.random.split(jax.random.key(seed), 19)
    return {
        "tokens": gaussian(splits[0], (SEQS, L, D), 1.0, 6.0, ((0, 32),)),
        "cotangent": gaussian_with(splits[1], (SEQS, L, D), 1.0, 6.0, ((0, 32),), (0, 2, 32, 2.75)),
        "lengths": draw_lengths(jax.random.fold_in(splits[18], 71), 0),
        "w_qkv": gaussian(splits[3], (D, 3 * D), D ** -0.5, 0.21875, ((0, 4),), jnp.float32),
        "w_out": gaussian(splits[4], (D, D), (max(9 * D // (2 * L), 1)) ** -0.5, 2.5, ((0, 4),), jnp.float32),
        "w_up": gaussian(splits[5], (D, FF), D ** -0.5, 0.21875, ((0, 4),), jnp.float32),
        "w_down": gaussian(splits[6], (FF, D), FF ** -0.5, 0.109375, ((0, 4),), jnp.float32),
        "vectors": draw_vectors(jax.random.fold_in(splits[18], 71), 0),
        "first_qkv": draw_first_qkv(jax.random.fold_in(splits[18], 71), 0),
        "first_out": draw_first_out(jax.random.fold_in(splits[18], 71), 0),
        "first_up": draw_first_up(jax.random.fold_in(splits[18], 71), 0),
        "first_down": draw_first_down(jax.random.fold_in(splits[18], 71), 0),
        "first_vectors": draw_first_vectors(jax.random.fold_in(splits[18], 71), 0),
        "second_qkv": draw_second_qkv(jax.random.fold_in(splits[18], 71), 0),
        "second_out": draw_second_out(jax.random.fold_in(splits[18], 71), 0),
        "second_up": draw_second_up(jax.random.fold_in(splits[18], 71), 0),
        "second_down": draw_second_down(jax.random.fold_in(splits[18], 71), 0),
        "second_vectors": draw_second_vectors(jax.random.fold_in(splits[18], 71), 0),
    }


@jax.custom_vjp
def low(v):
    return lax.optimization_barrier(v.astype(jnp.bfloat16)).astype(jnp.float32)

@jax.custom_vjp
def low_back(v):
    return v

def low_keep(v):
    return (low(v), None)

def low_pass(kept, grad):
    return (grad,)

def back_keep(v):
    return (v, None)

def back_low(kept, grad):
    return (low(grad),)
low.defvjp(low_keep, low_pass)
low_back.defvjp(back_keep, back_low)
EPS_NORM = 1e-05
EPS_ADAM = 1e-06
BETA_ONE = 0.9
BETA_TWO = 0.999
DECAY_RATE = 0.01
NEG_FILL = -1e+30

def dot_high(left, right):
    return jnp.dot(left, right, precision=lax.Precision.HIGHEST, preferred_element_type=jnp.float32)

def both_ways(value):
    return low_back(low(value))

def norm_rows(hidden, norm_gain, norm_shift):
    row_mean = lax.optimization_barrier(jnp.mean(hidden, axis=-1, keepdims=True))
    centred = hidden - row_mean
    row_var = lax.optimization_barrier(jnp.mean(centred * centred, axis=-1, keepdims=True))
    return centred * lax.rsqrt(row_var + EPS_NORM) * norm_gain + norm_shift

def attend_one(seq_item):
    queries, key_rows, value_rows, length = seq_item
    score_scale = 1.0 / math.sqrt(HEAD_DIM)
    raw_scores = low_back(jnp.einsum('qhd,khd->hqk', queries, key_rows, precision=lax.Precision.HIGHEST) * score_scale)
    valid = (jnp.arange(L, dtype=jnp.int32) < length)[None, None, :]
    scores = jnp.where(valid, raw_scores, NEG_FILL)
    row_top = lax.optimization_barrier(jnp.max(scores, axis=-1, keepdims=True))
    exponent = jnp.exp(scores - row_top)
    attn_prob = exponent / lax.optimization_barrier(jnp.sum(exponent, axis=-1, keepdims=True))
    return both_ways(jnp.einsum('hqk,khd->qhd', low(attn_prob), value_rows, precision=lax.Precision.HIGHEST))

def layer_group(inputs, seq_lengths, params):
    w_qkv, w_out, w_up, w_down, vectors = [low(item) for item in params]
    seq_count = inputs.shape[0]
    flat_tokens = inputs.reshape(seq_count * L, D)
    mixed_proj = dot_high(flat_tokens, w_qkv)
    queries = both_ways(mixed_proj[:, :D] + vectors[0])
    key_rows = both_ways(mixed_proj[:, D:2 * D])
    value_rows = both_ways(mixed_proj[:, 2 * D:] + vectors[1])
    head_shape = (seq_count, L, HEADS, HEAD_DIM)
    context = lax.map(jax.checkpoint(attend_one), (queries.reshape(head_shape), key_rows.reshape(head_shape), value_rows.reshape(head_shape), seq_lengths))
    attended = low_back(dot_high(context.reshape(seq_count * L, D), w_out) + vectors[2])
    first_norm = low(norm_rows(flat_tokens + attended, vectors[4], vectors[5]))
    upward = low_back(dot_high(first_norm, w_up) + vectors[8:12].reshape(FF))
    active = low(jax.nn.gelu(upward, approximate=False))
    branch = low_back(dot_high(active, w_down) + vectors[3])
    return norm_rows(first_norm + branch, vectors[6], vectors[7]).reshape(seq_count, L, D)

def step_rates():
    return (1.5 / math.sqrt(D), 1.5 / math.sqrt(max(9 * D // (2 * L), 1)), 1.5 / math.sqrt(D), 1.5 / math.sqrt(FF), 0.3)

def adam_update(weight, gradient, first_old, second_old, rate, decay):
    first_new = BETA_ONE * first_old + (1.0 - BETA_ONE) * gradient
    second_new = BETA_TWO * second_old + (1.0 - BETA_TWO) * gradient * gradient
    step_mean = first_new / (1.0 - BETA_ONE ** STEP)
    step_var = second_new / (1.0 - BETA_TWO ** STEP)
    weight_new = weight - rate * (step_mean / (jnp.sqrt(step_var) + EPS_ADAM) + decay * weight)
    return (weight_new, first_new, second_new)

def reference(tokens, cotangent, lengths, w_qkv, w_out, w_up, w_down, vectors, first_qkv, first_out, first_up, first_down, first_vectors, second_qkv, second_out, second_up, second_down, second_vectors):
    group_count = N_DP
    per_group = SEQS // group_count
    grouped_tokens = tokens.astype(jnp.float32).reshape(group_count, per_group, L, D)
    grouped_cot = cotangent.astype(jnp.float32).reshape(group_count, per_group, L, D)
    grouped_len = lengths.reshape(group_count, per_group)
    masters = (w_qkv, w_out, w_up, w_down, vectors)

    def scan_step(totals, seq_item):
        group_tokens, group_cot, group_len = seq_item
        valid = (jnp.arange(L, dtype=jnp.int32)[None, :] < group_len[:, None]).astype(jnp.float32)
        result, pull_back = jax.vjp(lambda inputs, params: layer_group(inputs, group_len, params), group_tokens, masters)
        back_in, back_params = pull_back(group_cot * valid[:, :, None])
        totals = jax.tree.map(jnp.add, totals, back_params)
        return (totals, (result, back_in))
    zeros_start = jax.tree.map(jnp.zeros_like, masters)
    gradients, (results, back_inputs) = lax.scan(scan_step, zeros_start, (grouped_tokens, grouped_cot, grouped_len))
    firsts = (first_qkv, first_out, first_up, first_down, first_vectors)
    seconds = (second_qkv, second_out, second_up, second_down, second_vectors)
    decays = (DECAY_RATE, DECAY_RATE, DECAY_RATE, DECAY_RATE, 0.0)
    updated = [adam_update(masters[index], gradients[index], firsts[index], seconds[index], step_rates()[index], decays[index]) for index in range(5)]
    return (results.reshape(SEQS, L, D), back_inputs.reshape(SEQS, L, D), gradients[0], gradients[1], gradients[2], gradients[3], gradients[4], updated[0][0], updated[1][0], updated[2][0], updated[3][0], updated[4][0], updated[0][1], updated[1][1], updated[2][1], updated[3][1], updated[4][1], updated[0][2], updated[1][2], updated[2][2], updated[3][2], updated[4][2])
```

```python
import math

import jax
import jax.numpy as jnp
from jax import lax
from jax.experimental import pallas as pl
from jax.experimental.pallas import tpu as pltpu
from jax.sharding import PartitionSpec as P

D = 768
HEADS = 12
HEAD_DIM = 64
FF = 3072
L = 512
STEP = 10

EPS_NORM = 1e-05
EPS_ADAM = 1e-06
BETA_ONE = 0.9
BETA_TWO = 0.999
DECAY_RATE = 0.01
NEG_FILL = -1e30

NN = (((1,), (0,)), ((), ()))
NT = (((1,), (1,)), ((), ()))
TN = (((0,), (0,)), ((), ()))
BF = jnp.bfloat16
F32 = jnp.float32

PAIR = 2 * HEAD_DIM
PAIRS = HEADS // 2
ROWS = 256
UP_COLS = 512

ERF_P = 0.39
ERF_C = (
    0.23532515294504244,
    0.09138882950769733,
    0.6495583643148856,
    -0.6353989981290624,
    0.8866635822029096,
    -0.2275369325376688,
)


def dot(left, right, dims):
    return lax.dot_general(left, right, dims, preferred_element_type=F32)


def gelu_and_slope(u):
    density = jnp.exp(u * u * -0.5)
    base = 1.0 + (ERF_P / math.sqrt(2.0)) * jnp.abs(u)
    t = pl.reciprocal(base, approx=True)
    t = t * (2.0 - base * t)
    poly = 0.5 * ERF_C[5]
    for coef in ERF_C[4::-1]:
        poly = poly * t + 0.5 * coef
    tail = poly * t * density
    phi_cdf = jnp.where(u < 0.0, tail, 1.0 - tail)
    return u * phi_cdf, phi_cdf + u * (density * (1.0 / math.sqrt(2.0 * math.pi)))


def norm_stats(hidden):
    row_mean = jnp.mean(hidden, axis=-1, keepdims=True)
    centred = hidden - row_mean
    row_var = jnp.mean(centred * centred, axis=-1, keepdims=True)
    inv = lax.rsqrt(row_var + EPS_NORM)
    return centred * inv, inv


def norm_back(grad, unit, inv, gain):
    scaled = grad * gain
    mean_one = jnp.mean(scaled, axis=-1, keepdims=True)
    mean_two = jnp.mean(scaled * unit, axis=-1, keepdims=True)
    return inv * (scaled - mean_one - unit * mean_two)


def add_row(ref, row, value, first):
    total = jnp.sum(value, axis=0, keepdims=True)

    @pl.when(first)
    def _():
        ref[row : row + 1, :] = total

    @pl.when(jnp.logical_not(first))
    def _():
        ref[row : row + 1, :] += total


def attend_forward_kernel(len_ref, q_ref, k_ref, v_ref, c_ref, p_ref):
    length = len_ref[pl.program_id(0)]
    queries, key_rows, value_rows = q_ref[...], k_ref[...], v_ref[...]
    lane_head = lax.broadcasted_iota(jnp.int32, key_rows.shape, 1) // HEAD_DIM
    key_scaled = key_rows * jnp.asarray(1.0 / math.sqrt(HEAD_DIM), BF)
    value_t = value_rows.T
    parts = []
    for head in range(2):
        key_one = jnp.where(lane_head == head, key_scaled, jnp.zeros_like(key_scaled))
        scores = dot(key_one, queries, NT)
        key_pos = lax.broadcasted_iota(jnp.int32, scores.shape, 0)
        scores = jnp.where(key_pos < length, scores, NEG_FILL)
        top = jnp.max(scores, axis=0, keepdims=True)
        exponent = jnp.exp(scores - top)
        total = jnp.sum(exponent, axis=0, keepdims=True)
        prob = (exponent * (1.0 / total)).astype(BF)
        p_ref[0, head] = prob
        parts.append(dot(value_t[head * HEAD_DIM : (head + 1) * HEAD_DIM], prob, NN))
    c_ref[...] = jnp.concatenate(parts, axis=0).T.astype(BF)


def attend_forward(lengths, mixed):
    seq_count = lengths.shape[0]
    width = mixed.shape[1] // 3
    pairs = width // PAIR
    block = lambda offset: pl.BlockSpec((L, PAIR), lambda s, p, n: (s, p + offset))
    return pl.pallas_call(
        attend_forward_kernel,
        grid_spec=pltpu.PrefetchScalarGridSpec(
            num_scalar_prefetch=1,
            grid=(seq_count, pairs),
            in_specs=[block(0), block(pairs), block(2 * pairs)],
            out_specs=[
                pl.BlockSpec((L, PAIR), lambda s, p, n: (s, p)),
                pl.BlockSpec((1, 2, L, L), lambda s, p, n: (s, p, 0, 0)),
            ],
        ),
        out_shape=[
            jax.ShapeDtypeStruct((seq_count * L, width), BF),
            jax.ShapeDtypeStruct((seq_count, 2 * pairs, L, L), BF),
        ],
        compiler_params=params(),
        cost_estimate=pl.CostEstimate(
            flops=seq_count * pairs * 8 * L * L * 256,
            bytes_accessed=seq_count * pairs * (4 * L * L + 8 * L * PAIR),
            transcendentals=seq_count * pairs * 2 * L * L,
        ),
        name="attend_forward",
    )(lengths, mixed, mixed, mixed)


def attend_backward_kernel(p_ref, q_ref, k_ref, v_ref, d_ref, b_ref):
    queries, key_rows, value_rows, d_context = q_ref[...], k_ref[...], v_ref[...], d_ref[...]
    lane_head = lax.broadcasted_iota(jnp.int32, key_rows.shape, 1) // HEAD_DIM
    scale = jnp.asarray(1.0 / math.sqrt(HEAD_DIM), BF)
    query_scaled = queries * scale
    key_t = (key_rows * scale).T
    parts = []
    d_keys = None
    d_values = None
    for head in range(2):
        own = lane_head == head
        pick = lambda rows: jnp.where(own, rows, jnp.zeros_like(rows))
        prob = p_ref[0, head]
        d_prob = dot(pick(value_rows), d_context, NT)
        one_value = dot(prob, pick(d_context), NN)
        prob_wide = prob.astype(F32)
        weighted = prob_wide * d_prob
        delta = jnp.sum(weighted, axis=0, keepdims=True)
        d_scores = (weighted - prob_wide * delta).astype(BF)
        one_key = dot(d_scores, pick(query_scaled), NN)
        parts.append(dot(key_t[head * HEAD_DIM : (head + 1) * HEAD_DIM], d_scores, NN))
        d_keys = one_key if d_keys is None else d_keys + one_key
        d_values = one_value if d_values is None else d_values + one_value
    b_ref[0] = jnp.concatenate(parts, axis=0).T.astype(BF)
    b_ref[1] = d_keys.astype(BF)
    b_ref[2] = d_values.astype(BF)


def attend_backward(prob, mixed, d_context, chunk):
    rows, width = mixed.shape
    seq_count = rows // L
    pairs = width // (3 * PAIR)
    block = lambda offset: pl.BlockSpec((L, PAIR), lambda s, p: (s, p + offset))
    return pl.pallas_call(
        attend_backward_kernel,
        grid=(seq_count, pairs),
        in_specs=[
            pl.BlockSpec((1, 2, L, L), lambda s, p: (s, p, 0, 0)),
            block(0),
            block(pairs),
            block(2 * pairs),
            block(chunk * pairs),
        ],
        out_specs=pl.BlockSpec((3, L, PAIR), lambda s, p: (0, s, p)),
        out_shape=jax.ShapeDtypeStruct((3, rows, pairs * PAIR), BF),
        compiler_params=params(),
        cost_estimate=pl.CostEstimate(
            flops=seq_count * pairs * 20 * L * L * 256,
            bytes_accessed=seq_count * pairs * (4 * L * L + 16 * L * PAIR),
            transcendentals=0,
        ),
        name="attend_backward",
    )(prob, mixed, mixed, mixed, d_context)


ANY = pl.BlockSpec(memory_space=pl.ANY)
VEC_ROWS = 16
VEC_PAD = 128


def params(mebibytes=56):
    return pltpu.CompilerParams(vmem_limit_bytes=mebibytes * 1024 * 1024)


def block_copies(blocks, whole, sems):
    own = lax.axis_index("zero")
    low = lax.axis_index("dp") & 1
    rows = blocks[0][0].shape[0]
    copies = []
    for place, parts in enumerate(blocks):
        start = (own ^ place) * rows
        for index, part in enumerate(parts):
            size = part.shape[0]
            offset = start if len(parts) == 1 else start + (low ^ index) * size
            target = whole.at[pl.ds(pl.multiple_of(offset, 16), size), :]
            copies.append(pltpu.make_async_copy(part, target, sems.at[len(copies)]))
    return copies


def flat(blocks):
    return [part for parts in blocks for part in parts]


def like(blocks, refs):
    refs = iter(refs)
    return [[next(refs) for _ in parts] for parts in blocks]


def load_now(first, copies):
    @pl.when(first)
    def _():
        for copy in copies:
            copy.start()
        for copy in copies:
            copy.wait()


def project_kernel(blocks, has_vec, *refs):
    count = len(flat(blocks))
    x_ref, v_in = refs[0], None if has_vec else refs[1]
    refs = refs[1 if has_vec else 2 :]
    parts = like(blocks, refs[:count])
    mixed_ref = refs[count]
    vec_ref = refs[count + 1] if has_vec else v_in
    whole, sems = refs[-2:]
    first = pl.program_id(0) == 0
    load_now(first, block_copies(parts, whole, sems))
    width = mixed_ref.shape[1] // 3
    if has_vec:

        @pl.when(first)
        def _():
            vec_ref[...] = whole[:, 3 * width :].astype(F32).T[:VEC_ROWS]

    start = 0 if has_vec else D - width
    for part in range(3):
        cols = slice(part * width, (part + 1) * width)
        value = dot(x_ref[...], whole[:, cols], NN)
        if part != 1:
            value = value + vec_ref[part // 2 : part // 2 + 1, start : start + width]
        mixed_ref[:, cols] = value.astype(BF)


def project(tokens, blocks, vec):
    rows = tokens.shape[0]
    count = len(flat(blocks))
    has_vec = vec is None
    columns = blocks[0][0].shape[1]
    width = columns - (VEC_PAD if has_vec else 0)
    small = pl.BlockSpec((VEC_ROWS, D), lambda i: (0, 0))
    out_specs = [pl.BlockSpec((L, width), lambda i: (i, 0))]
    out_shape = [jax.ShapeDtypeStruct((rows, width), BF)]
    if has_vec:
        out_specs.append(small)
        out_shape.append(jax.ShapeDtypeStruct((VEC_ROWS, D), F32))
    return pl.pallas_call(
        lambda *refs: project_kernel(blocks, has_vec, *refs),
        grid=(rows // L,),
        in_specs=[pl.BlockSpec((L, D), lambda i: (i, 0))] + ([] if has_vec else [small]) + [ANY] * count,
        out_specs=out_specs,
        out_shape=out_shape,
        scratch_shapes=[pltpu.VMEM((D, columns), BF), pltpu.SemaphoreType.DMA((count,))],
        compiler_params=params(),
        cost_estimate=pl.CostEstimate(
            flops=2 * rows * D * width, bytes_accessed=rows * (D + width) * 2 + D * width * 2, transcendentals=0
        ),
        name="project",
    )(tokens, *(() if has_vec else (vec,)), *flat(blocks))


def out_kernel(blocks, chunks, *refs):
    count = len(flat(blocks))
    c_refs, (x_ref, v_ref) = refs[:chunks], refs[chunks : chunks + 2]
    parts = like(blocks, refs[chunks + 2 : chunks + 2 + count])
    h_ref, n_ref, whole, sems = refs[chunks + 2 + count :]
    load_now(pl.program_id(0) == 0, block_copies(parts, whole, sems))
    context = jnp.concatenate([c_ref[...] for c_ref in c_refs], axis=1)
    hidden = x_ref[...].astype(F32) + (dot(context, whole[...], NN) + v_ref[2:3])
    h_ref[...] = hidden
    unit, _ = norm_stats(hidden)
    n_ref[...] = (unit * v_ref[4:5] + v_ref[5:6]).astype(BF)


def out_norm(contexts, tokens, vec, blocks):
    rows = tokens.shape[0]
    count = len(flat(blocks))
    chunks = len(contexts)
    row = pl.BlockSpec((ROWS, D), lambda i: (i, 0))
    return pl.pallas_call(
        lambda *refs: out_kernel(blocks, chunks, *refs),
        grid=(rows // ROWS,),
        in_specs=[pl.BlockSpec((ROWS, context.shape[1]), lambda i: (i, 0)) for context in contexts]
        + [row, pl.BlockSpec((VEC_ROWS, D), lambda i: (0, 0))]
        + [ANY] * count,
        out_specs=[row, row],
        out_shape=[jax.ShapeDtypeStruct((rows, D), F32), jax.ShapeDtypeStruct((rows, D), BF)],
        scratch_shapes=[pltpu.VMEM((D, D), BF), pltpu.SemaphoreType.DMA((count,))],
        compiler_params=params(),
        cost_estimate=pl.CostEstimate(
            flops=2 * rows * D * D, bytes_accessed=rows * D * 10 + D * D * 2, transcendentals=0
        ),
        name="out_norm",
    )(*contexts, tokens, vec, *flat(blocks))


def flip_kernel(x_ref, o_ref, flipped):
    relative_rows(x_ref[...], (flipped, o_ref))


def flip_tokens(tokens):
    rows = tokens.shape[0]
    return pl.pallas_call(
        flip_kernel,
        out_shape=jax.ShapeDtypeStruct((D, rows), BF),
        scratch_shapes=[pltpu.VMEM((D, rows), BF)],
        compiler_params=params(),
        name="flip_tokens",
    )(tokens)


def up_kernel(blocks, *refs):
    count = len(flat(blocks))
    n_ref, b_ref = refs[:2]
    parts = like(blocks, refs[2 : 2 + count])
    g_ref, s_ref, whole, sems = refs[2 + count :]
    load_now(pl.program_id(0) == 0, block_copies(parts, whole, sems))
    cols = pl.ds(pl.multiple_of(pl.program_id(0) * UP_COLS, UP_COLS), UP_COLS)
    weight = whole[:, cols]
    bias = b_ref[...]
    for start in range(0, n_ref.shape[0], ROWS):
        part = slice(start, start + ROWS)
        active, slope = gelu_and_slope(dot(n_ref[part, :], weight, NN) + bias)
        g_ref[part, :] = active.astype(BF)
        s_ref[part, :] = slope


def up_gelu(first_low, bias, blocks):
    rows = first_low.shape[0]
    count = len(flat(blocks))
    column = pl.BlockSpec((rows, UP_COLS), lambda j: (0, j))
    return pl.pallas_call(
        lambda *refs: up_kernel(blocks, *refs),
        grid=(FF // UP_COLS,),
        in_specs=[pl.BlockSpec((rows, D), lambda j: (0, 0)), pl.BlockSpec((1, UP_COLS), lambda j: (0, j))]
        + [ANY] * count,
        out_specs=[column, column],
        out_shape=[jax.ShapeDtypeStruct((rows, FF), BF), jax.ShapeDtypeStruct((rows, FF), F32)],
        scratch_shapes=[pltpu.VMEM((D, FF), BF), pltpu.SemaphoreType.DMA((count,))],
        compiler_params=params(),
        cost_estimate=pl.CostEstimate(
            flops=2 * rows * D * FF, bytes_accessed=rows * FF * 6 + D * FF * 2, transcendentals=2 * rows * FF
        ),
        name="up_gelu",
    )(first_low, bias, *flat(blocks))


def down_kernel(blocks, *refs):
    count = len(flat(blocks))
    len_ref, g_ref, n_ref, t_ref, v_ref = refs[:5]
    parts = like(blocks, refs[5 : 5 + count])
    o_ref, h_ref, m_ref, s_ref, whole, sems = refs[5 + count :]
    step = pl.program_id(0)
    first = step == 0
    load_now(first, block_copies(parts, whole, sems))
    per_slot = L // ROWS
    length = len_ref[step // per_slot]
    hidden = n_ref[...].astype(F32) + (dot(g_ref[...], whole[...], NN) + v_ref[3:4])
    unit, inv = norm_stats(hidden)
    gain = v_ref[6:7]
    o_ref[...] = unit * gain + v_ref[7:8]
    position = (step % per_slot) * ROWS + lax.broadcasted_iota(jnp.int32, hidden.shape, 0)
    out_grad = jnp.where(position < length, t_ref[...].astype(F32), 0.0)
    d_hidden = norm_back(out_grad, unit, inv, gain)
    h_ref[...] = d_hidden
    d_low = d_hidden.astype(BF)
    m_ref[...] = d_low
    add_row(s_ref, 0, d_low.astype(F32), first)
    add_row(s_ref, 1, out_grad * unit, first)
    add_row(s_ref, 2, out_grad, first)


def down_norm(lengths, active, first_low, cotangent, vec, blocks):
    rows = active.shape[0]
    count = len(flat(blocks))
    row = pl.BlockSpec((ROWS, D), lambda i, n: (i, 0))
    return pl.pallas_call(
        lambda *refs: down_kernel(blocks, *refs),
        grid_spec=pltpu.PrefetchScalarGridSpec(
            num_scalar_prefetch=1,
            grid=(rows // ROWS,),
            in_specs=[
                pl.BlockSpec((ROWS, FF), lambda i, n: (i, 0)),
                row,
                row,
                pl.BlockSpec((VEC_ROWS, D), lambda i, n: (0, 0)),
            ]
            + [ANY] * count,
            out_specs=[row, row, row, pl.BlockSpec((8, D), lambda i, n: (0, 0))],
            scratch_shapes=[pltpu.VMEM((FF, D), BF), pltpu.SemaphoreType.DMA((count,))],
        ),
        out_shape=[
            jax.ShapeDtypeStruct((rows, D), F32),
            jax.ShapeDtypeStruct((rows, D), F32),
            jax.ShapeDtypeStruct((rows, D), BF),
            jax.ShapeDtypeStruct((8, D), F32),
        ],
        compiler_params=params(),
        cost_estimate=pl.CostEstimate(
            flops=2 * rows * D * FF, bytes_accessed=rows * (FF * 2 + D * 14) + D * FF * 2, transcendentals=0
        ),
        name="down_norm",
    )(lengths, active, first_low, cotangent, vec, *flat(blocks))


def slope_kernel(blocks, *refs):
    count = len(flat(blocks))
    m_ref, s_ref = refs[:2]
    parts = like(blocks, refs[2 : 2 + count])
    u_ref, bias_ref, whole, sems = refs[2 + count :]
    load_now(pl.program_id(0) == 0, block_copies(parts, whole, sems))
    rows = pl.ds(pl.multiple_of(pl.program_id(0) * UP_COLS, UP_COLS), UP_COLS)
    d_up = (dot(m_ref[...], whole[rows, :], NT) * s_ref[...]).astype(BF)
    u_ref[...] = d_up
    bias_ref[...] = jnp.sum(d_up.astype(F32), axis=0, keepdims=True)


def slope_back(d_branch, slope, blocks):
    rows = d_branch.shape[0]
    count = len(flat(blocks))
    column = pl.BlockSpec((rows, UP_COLS), lambda j: (0, j))
    return pl.pallas_call(
        lambda *refs: slope_kernel(blocks, *refs),
        grid=(FF // UP_COLS,),
        in_specs=[pl.BlockSpec((rows, D), lambda j: (0, 0)), column] + [ANY] * count,
        out_specs=[column, pl.BlockSpec((1, UP_COLS), lambda j: (0, j))],
        out_shape=[jax.ShapeDtypeStruct((rows, FF), BF), jax.ShapeDtypeStruct((1, FF), F32)],
        scratch_shapes=[pltpu.VMEM((FF, D), BF), pltpu.SemaphoreType.DMA((count,))],
        compiler_params=params(),
        cost_estimate=pl.CostEstimate(
            flops=2 * rows * D * FF, bytes_accessed=rows * (FF * 6 + D * 2) + D * FF * 2, transcendentals=0
        ),
        name="slope_back",
    )(d_branch, slope, *flat(blocks))


def back_kernel(up_blocks, out_blocks, *refs):
    u_ref, dh_ref, h_ref, v_ref = refs[:4]
    ups, outs = len(flat(up_blocks)), len(flat(out_blocks))
    up_parts = like(up_blocks, refs[4 : 4 + ups])
    out_parts = like(out_blocks, refs[4 + ups : 4 + ups + outs])
    r_ref, a_ref, c_ref, sum_ref, up, out, up_sems, out_sems = refs[4 + ups + outs :]
    first = pl.program_id(0) == 0
    load_now(first, block_copies(up_parts, up, up_sems) + block_copies(out_parts, out, out_sems))
    d_first = dh_ref[...] + dot(u_ref[...], up[...], NT)
    unit, inv = norm_stats(h_ref[...])
    d_resid = norm_back(d_first, unit, inv, v_ref[4:5])
    r_ref[...] = d_resid
    d_attended = d_resid.astype(BF)
    a_ref[...] = d_attended
    c_ref[...] = dot(d_attended, out[...], NT).astype(BF)
    add_row(sum_ref, 0, d_attended.astype(F32), first)
    add_row(sum_ref, 1, d_first * unit, first)
    add_row(sum_ref, 2, d_first, first)


def back_rows(d_upward, d_second, hidden, vec, ups, outs):
    rows = d_upward.shape[0]
    counts = len(flat(ups)), len(flat(outs))
    row = pl.BlockSpec((ROWS, D), lambda i: (i, 0))
    whole = lambda *shape: pl.BlockSpec(shape, lambda i: (0, 0))
    return pl.pallas_call(
        lambda *refs: back_kernel(ups, outs, *refs),
        grid=(rows // ROWS,),
        in_specs=[pl.BlockSpec((ROWS, FF), lambda i: (i, 0)), row, row, whole(VEC_ROWS, D)] + [ANY] * sum(counts),
        out_specs=[row, row, row, whole(8, D)],
        out_shape=[
            jax.ShapeDtypeStruct((rows, D), F32),
            jax.ShapeDtypeStruct((rows, D), BF),
            jax.ShapeDtypeStruct((rows, D), BF),
            jax.ShapeDtypeStruct((8, D), F32),
        ],
        scratch_shapes=[
            pltpu.VMEM((D, FF), BF),
            pltpu.VMEM((D, D), BF),
            pltpu.SemaphoreType.DMA((counts[0],)),
            pltpu.SemaphoreType.DMA((counts[1],)),
        ],
        compiler_params=params(),
        cost_estimate=pl.CostEstimate(
            flops=rows * (2 * D * FF + 2 * D * D),
            bytes_accessed=rows * (FF * 2 + D * 18) + D * FF * 2,
            transcendentals=0,
        ),
        name="back_rows",
    )(d_upward, d_second, hidden, vec, *flat(ups), *flat(outs))


def input_kernel(groups, *refs):
    chunks = len(groups)
    r_ref, backs, refs = refs[0], refs[1 : 1 + chunks], refs[1 + chunks :]
    parts = []
    for blocks in groups:
        count = len(flat(blocks))
        parts.append(like(blocks, refs[:count]))
        refs = refs[count:]
    o_ref, wholes, sems = refs[0], refs[1 : 1 + chunks], refs[1 + chunks :]
    copies = [copy for item in zip(parts, wholes, sems) for copy in block_copies(*item)]
    load_now(pl.program_id(0) == 0, copies)
    total = r_ref[...]
    for back, whole in zip(backs, wholes):
        width = back.shape[2]
        for part in range(3):
            total = total + dot(back[part], whole[:, part * width : (part + 1) * width], NT)
    o_ref[...] = total


def input_gradient(d_resid, backs, groups):
    rows = d_resid.shape[0]
    row = pl.BlockSpec((ROWS, D), lambda i: (i, 0))
    counts = [len(flat(blocks)) for blocks in groups]
    return pl.pallas_call(
        lambda *refs: input_kernel(groups, *refs),
        grid=(rows // ROWS,),
        in_specs=[row]
        + [pl.BlockSpec((3, ROWS, back.shape[2]), lambda i: (0, i, 0)) for back in backs]
        + [ANY] * sum(counts),
        out_specs=row,
        out_shape=jax.ShapeDtypeStruct((rows, D), F32),
        scratch_shapes=[pltpu.VMEM((D, blocks[0][0].shape[1]), BF) for blocks in groups]
        + [pltpu.SemaphoreType.DMA((count,)) for count in counts],
        compiler_params=params(),
        cost_estimate=pl.CostEstimate(
            flops=6 * rows * D * D, bytes_accessed=rows * D * 14 + D * D * 6, transcendentals=0
        ),
        name="input_gradient",
    )(d_resid, *backs, *(part for blocks in groups for part in flat(blocks)))


def relative_rows(left, scratch):
    count = lax.axis_size("zero")
    own = lax.axis_index("zero")
    flipped, ordered = scratch
    flipped[...] = left.T
    rows = flipped.shape[0] // count
    for place in range(count):
        slot = place // 2 + (place % 2) * (count // 2)
        start = pl.multiple_of((own ^ place) * rows, 16)
        ordered[slot * rows : (slot + 1) * rows, :] = flipped[pl.ds(start, rows), :]


def split_store(value, keep_ref, send_ref, cols):
    low_value = value.astype(BF).reshape(2, keep_ref.shape[0], -1, value.shape[1])
    keep_ref[:, :, cols] = low_value[0]
    send_ref[:, :, cols] = low_value[1]


def down_grad_kernel(own_ref, g_ref, d_ref, send_ref, keep_ref):
    value = dot(g_ref[...], d_ref[...], TN).astype(BF)
    half = pl.num_programs(0) // 2

    @pl.when(pl.program_id(0) < half)
    def _():
        send_ref[0] = value

    @pl.when(pl.program_id(0) >= half)
    def _():
        keep_ref[0] = value


def down_grad(active, d_branch):
    rows = active.shape[0]
    count = lax.axis_size("zero")
    half = count // 2
    width = FF // count
    own = lax.axis_index("zero").astype(jnp.int32).reshape(1)

    def place(i, own):
        return (0, own[0] ^ jnp.where(i < half, 2 * i + 1, 2 * (i - half)))

    return pl.pallas_call(
        down_grad_kernel,
        grid_spec=pltpu.PrefetchScalarGridSpec(
            num_scalar_prefetch=1,
            grid=(count,),
            in_specs=[
                pl.BlockSpec((rows, width), place),
                pl.BlockSpec((rows, D), lambda i, own: (0, 0)),
            ],
            out_specs=[
                pl.BlockSpec((1, width, D), lambda i, own: (jnp.minimum(i, half - 1), 0, 0)),
                pl.BlockSpec((1, width, D), lambda i, own: (jnp.maximum(i - half, 0), 0, 0)),
            ],
        ),
        out_shape=[jax.ShapeDtypeStruct((half, width, D), BF)] * 2,
        compiler_params=params(),
        cost_estimate=pl.CostEstimate(
            flops=2 * rows * D * FF, bytes_accessed=rows * (FF + D) * 2 + D * FF * 2, transcendentals=0
        ),
        name="down_grad",
    )(own, active, d_branch)


MID_COLS = 384


def up_grad_kernel(n_ref, u_ref, send_ref, keep_ref, flipped, ordered):
    @pl.when(pl.program_id(0) == 0)
    def _():
        relative_rows(n_ref[...], (flipped, ordered))

    split_store(dot(ordered[...], u_ref[...], NN), keep_ref, send_ref, slice(None))


def up_grad(first_low, d_upward):
    rows = first_low.shape[0]
    count = lax.axis_size("zero")
    result = pl.BlockSpec((count // 2, D // count, UP_COLS), lambda j: (0, 0, j))
    return pl.pallas_call(
        up_grad_kernel,
        grid=(FF // UP_COLS,),
        in_specs=[
            pl.BlockSpec((rows, D), lambda j: (0, 0)),
            pl.BlockSpec((rows, UP_COLS), lambda j: (0, j)),
        ],
        out_specs=[result, result],
        out_shape=[jax.ShapeDtypeStruct((count // 2, D // count, FF), BF)] * 2,
        scratch_shapes=[pltpu.VMEM((D, rows), BF), pltpu.VMEM((D, rows), BF)],
        compiler_params=params(),
        cost_estimate=pl.CostEstimate(
            flops=2 * rows * D * FF, bytes_accessed=rows * (FF + D) * 2 + D * FF * 2, transcendentals=0
        ),
        name="up_grad",
    )(first_low, d_upward)


def qkv_grad_kernel(chunks, tail, *refs):
    x_ref, b_ref = refs[:2]
    width = b_ref.shape[2]
    if tail:
        sums = refs[2]
        send_ref, keep_ref = refs[3:]
    else:
        contexts, a_ref = refs[2 : 2 + chunks], refs[2 + chunks]
        send_ref, keep_ref, flipped, ordered = refs[3 + chunks :]
    for part in range(3):
        split_store(
            dot(x_ref[...], b_ref[part], NN), keep_ref, send_ref, slice(part * width, (part + 1) * width)
        )
    if tail:
        count = lax.axis_size("zero")
        own = lax.axis_index("zero")
        rows = D // count
        for place in range(count):
            start = pl.multiple_of((own ^ place) * rows, 16)
            target = (keep_ref, send_ref)[place % 2]
            target[place // 2, :, 3 * width :] = sums[pl.ds(start, rows), :]
    else:
        relative_rows(jnp.concatenate([c_ref[...] for c_ref in contexts], axis=1), (flipped, ordered))
        split_store(dot(ordered[...], a_ref[...], NN), keep_ref, send_ref, slice(3 * width, 3 * width + D))


def qkv_grad(flipped_tokens, back, sums=None, contexts=(), d_attended=None):
    rows = flipped_tokens.shape[1]
    count = lax.axis_size("zero")
    tail = sums is not None
    width = 3 * back.shape[2] + (VEC_PAD if tail else D)
    more = (sums,) if tail else (*contexts, d_attended)
    return pl.pallas_call(
        lambda *refs: qkv_grad_kernel(len(contexts), tail, *refs),
        out_shape=[jax.ShapeDtypeStruct((count // 2, D // count, width), BF)] * 2,
        scratch_shapes=[] if tail else [pltpu.VMEM((D, rows), BF), pltpu.VMEM((D, rows), BF)],
        compiler_params=params(),
        cost_estimate=pl.CostEstimate(
            flops=2 * rows * D * width, bytes_accessed=rows * (D + width) * 2 + D * width * 2, transcendentals=0
        ),
        name="qkv_grad",
    )(flipped_tokens, back, *more)


def swap_bit(value, axis_name, bit):
    count = lax.axis_size(axis_name)
    return lax.ppermute(value, axis_name, [(i, i ^ (1 << bit)) for i in range(count)])


def own_bit(axis_name, bit):
    return (lax.axis_index(axis_name) >> bit) & 1


def bit_count(axis_name):
    return lax.axis_size(axis_name).bit_length() - 1


def after(value, *others):
    others = tuple(other for other in others if other is not None)
    return lax.optimization_barrier((value, *others))[0] if others else value


class Gather:
    def __init__(self, shard, halves=True):
        self.shard = shard
        self.halves = halves and bit_count("dp") > 0
        if self.halves:
            half = shard.shape[0] // 2
            shard = lax.dynamic_slice_in_dim(shard, own_bit("dp", 0) * half, half, 0)
        self.sent = shard
        self.bits = bit_count("zero")
        self.direct = {0: shard}
        if self.bits > 1:
            self.direct[1 << self.bits - 1] = swap_bit(shard, "zero", self.bits - 1)

    def forward(self, wait):
        direct = {place: after(part, wait) if place else part for place, part in self.direct.items()}
        for bit in reversed(range(1, self.bits - 1)):
            for place in list(direct):
                direct[place | 1 << bit] = swap_bit(direct[place], "zero", bit)
        self.held = {place: [part] for place, part in direct.items() if place}
        for parts in self.held.values():
            self.sent = parts[0]
            if self.halves:
                parts.append(swap_bit(parts[0], "dp", 0))

    def finish(self, wait=None):
        if self.halves:
            self.held = {place: [parts[0], after(parts[1], wait)] for place, parts in self.held.items()}
        self.held[0] = [self.shard]
        for place in list(self.held):
            self.held[place | 1] = [swap_bit(part, "zero", 0) for part in self.held[place]]
        return [self.held[place] for place in range(len(self.held))]


def add_low(left, right):
    return (left.astype(F32) + right.astype(F32)).astype(BF)


def reduce_steps(send, keep, scatter_bits):
    moved = swap_bit(send, "zero", 0)
    got = after(moved, (yield send))
    for bit in reversed(range(1, bit_count("zero"))):
        half = keep.shape[0] // 2
        send = add_low(keep[half:], got[half:])
        moved = swap_bit(send, "zero", bit)
        keep = add_low(keep[:half], got[:half])
        got = after(moved, (yield send))
    keep, got = keep[0], got[0]
    for bit in range(scatter_bits):
        mine = own_bit("dp", bit)
        half = keep.shape[0] // 2
        cut = lambda value, which: lax.dynamic_slice_in_dim(value, which * half, half, 0)
        send = add_low(cut(keep, 1 - mine), cut(got, 1 - mine))
        moved = swap_bit(send, "dp", bit)
        keep = add_low(cut(keep, mine), cut(got, mine))
        got = after(moved, (yield send))
    held = add_low(keep, got)
    for bit in range(scatter_bits, bit_count("dp")):
        moved = swap_bit(held, "dp", bit)
        held = add_low(held, after(moved, (yield held)))
    pieces = {0: held}
    for bit in reversed(range(scatter_bits)):
        places = list(pieces)
        moved = {place: swap_bit(pieces[place], "dp", bit) for place in places}
        wait = yield pieces[places[-1]]
        for place in places:
            pieces[place | 1 << bit] = after(moved[place], wait)
    return [pieces[place] for place in range(len(pieces))]


class Chain:
    def __init__(self, send, keep, scatter_bits):
        self.steps = reduce_steps(send, keep, scatter_bits)
        self.result = None
        self.sent = next(self.steps)

    def step(self, wait=None):
        if self.result is None:
            try:
                self.sent = self.steps.send(wait)
            except StopIteration as stop:
                self.result = stop.value
        return self.result is None

    def finish(self):
        while self.step():
            pass
        return self.result


def in_order(pieces, scatter_bits):
    ordered = []
    own = lax.axis_index("dp") & ((1 << scatter_bits) - 1)
    stacked = jnp.stack(pieces)
    for place in range(len(pieces)):
        index = sum(((place >> bit) & 1) << (scatter_bits - 1 - bit) for bit in range(scatter_bits))
        ordered.append((index, stacked[own ^ place]))
    return jnp.concatenate([item for _, item in sorted(ordered, key=lambda pair: pair[0])], axis=0)


def step_rates():
    return (
        1.5 / math.sqrt(D),
        1.5 / math.sqrt(max(9 * D // (2 * L), 1)),
        1.5 / math.sqrt(D),
        1.5 / math.sqrt(FF),
        0.3,
    )


def adam_update(weight, gradient, first_old, second_old, rate, decay):
    first_new = BETA_ONE * first_old + (1.0 - BETA_ONE) * gradient
    second_new = BETA_TWO * second_old + (1.0 - BETA_TWO) * gradient * gradient
    step_mean = first_new * (1.0 / (1.0 - BETA_ONE**STEP))
    step_var = second_new * (1.0 / (1.0 - BETA_TWO**STEP))
    weight_new = weight - rate * (step_mean / (jnp.sqrt(step_var) + EPS_ADAM) + decay * weight)
    return (weight_new, first_new, second_new)


def adam_kernel(count, chunks, cuts, rate, own_ref, *refs):
    pieces = refs[: count * chunks]
    w_ref, m_ref, v_ref, g_out, w_out, m_out, v_out = refs[count * chunks :]
    for place in range(count):

        @pl.when(pl.program_id(0) // cuts == place)
        def _(place=place):
            group = pieces[place * chunks : (place + 1) * chunks]
            if chunks == 1:
                gradient = group[0][...].astype(F32)
            else:
                width = D // chunks
                gradient = jnp.concatenate(
                    [group[c][:, t * width : (t + 1) * width].astype(F32) for t in range(3) for c in range(chunks)],
                    axis=1,
                )
            g_out[...] = gradient
            w_out[...], m_out[...], v_out[...] = adam_update(
                w_ref[...], gradient, m_ref[...], v_ref[...], rate, DECAY_RATE
            )


def adam(groups, column, width, weight, first_old, second_old, rate, scatter_bits):
    chunks = len(groups)
    count = len(groups[0])
    rows, columns = weight.shape
    piece_rows = rows // count
    cuts = 1
    while piece_rows % (cuts * 32) == 0 and cuts < 1:
        cuts *= 2
    block_rows = piece_rows // cuts
    own = (lax.axis_index("dp") & (count - 1)).astype(jnp.int32).reshape(1)

    def place(i, own):
        mine = own[0] ^ (i // cuts)
        index = 0
        for bit in range(scatter_bits):
            index = index | ((mine >> bit) & 1) << (scatter_bits - 1 - bit)
        return (index * cuts + i % cuts, 0)

    row = pl.BlockSpec((block_rows, columns), place)

    def piece(place):
        return pl.BlockSpec(
            (block_rows, width), lambda i, own: (jnp.clip(i - place * cuts, 0, cuts - 1), column)
        )

    return pl.pallas_call(
        lambda *refs: adam_kernel(count, chunks, cuts, rate, *refs),
        grid_spec=pltpu.PrefetchScalarGridSpec(
            num_scalar_prefetch=1,
            grid=(count * cuts,),
            in_specs=[piece(place) for place in range(count) for _ in range(chunks)] + [row] * 3,
            out_specs=[row] * 4,
        ),
        out_shape=[jax.ShapeDtypeStruct(weight.shape, F32)] * 4,
        compiler_params=params(),
        cost_estimate=pl.CostEstimate(
            flops=20 * rows * columns, bytes_accessed=rows * columns * 30, transcendentals=rows * columns
        ),
        name="adam",
    )(own, *(group[place] for place in range(count) for group in groups), weight, first_old, second_old)


CHUNKS = 2
SCATTER_BITS = 2


def body(
    tokens,
    cotangent,
    lengths,
    w_qkv,
    w_out,
    w_up,
    w_down,
    vectors,
    first_qkv,
    first_out,
    first_up,
    first_down,
    first_vectors,
    second_qkv,
    second_out,
    second_up,
    second_down,
    second_vectors,
):
    seq_count, seq_len, feature = tokens.shape
    row_count = seq_count * seq_len
    flat_tokens = tokens.reshape(row_count, feature)
    scatter_bits = min(SCATTER_BITS, bit_count("dp"))
    while w_qkv.shape[0] % (16 << scatter_bits):
        scatter_bits -= 1

    low_qkv = w_qkv.astype(BF)
    width = feature // CHUNKS
    pick = lambda chunk: [
        low_qkv[:, part * feature + chunk * width : part * feature + (chunk + 1) * width] for part in range(3)
    ]
    vector_columns = jnp.pad(vectors.astype(BF).T, ((0, 0), (0, VEC_PAD - vectors.shape[0])))
    first_heads = Gather(jnp.concatenate([*pick(0), vector_columns], axis=1), halves=False)
    flipped = flip_tokens(flat_tokens)
    first_heads.forward(flipped)
    last_heads = Gather(after(jnp.concatenate(pick(1), axis=1), first_heads.sent), halves=False)
    blocks_0 = first_heads.finish()
    mixed_0, vec = project(after(flat_tokens, last_heads.sent), blocks_0, None)
    last_heads.forward(mixed_0)
    outs = Gather(after(w_out.astype(BF), last_heads.sent))
    upper = Gather(after(w_up.astype(BF), last_heads.sent))
    context_0, prob_0 = attend_forward(lengths, after(mixed_0, outs.sent, upper.sent))
    outs.forward(context_0)
    blocks_1 = last_heads.finish()
    (mixed_1,) = project(after(flat_tokens, outs.sent), blocks_1, vec)
    qkv_blocks = [blocks_0, blocks_1]
    upper.forward(mixed_1)
    lower = Gather(after(w_down.astype(BF), upper.sent))
    context_1, prob_1 = attend_forward(lengths, after(mixed_1, upper.sent, lower.sent))
    out_blocks = outs.finish(mixed_1)
    up_blocks = upper.finish(context_1)
    contexts, probs, mixeds = (context_0, context_1), (prob_0, prob_1), (mixed_0, mixed_1)
    hidden, first_low = out_norm(contexts, flat_tokens, vec, out_blocks)
    lower.forward(first_low)
    first_low = after(first_low, lower.sent)
    active, slope = up_gelu(first_low, vec[8:12].reshape(1, FF), up_blocks)
    down_blocks = lower.finish(active)
    output, d_second, d_branch, sums_two = down_norm(
        lengths, active, first_low, cotangent.reshape(row_count, feature), vec, down_blocks
    )
    downs = Chain(*down_grad(active, d_branch), scatter_bits)
    downs.step()
    d_upward, up_bias = slope_back(after(d_branch, downs.sent), slope, down_blocks)
    up_send, up_keep = up_grad(first_low, d_upward)
    downs.step(up_send)
    ups = Chain(after(up_send, downs.sent), up_keep, scatter_bits)
    ups.step()
    d_resid, d_attended, d_context, sums_one = back_rows(
        after(d_upward, downs.sent, ups.sent), d_second, hidden, vec, up_blocks, out_blocks
    )
    downs.step(d_attended)
    back_0 = attend_backward(prob_0, mixed_0, after(d_context, downs.sent), 0)
    downs.step(back_0)
    ups.step(back_0)
    pair_0 = qkv_grad(after(flipped, downs.sent, ups.sent), back_0, None, contexts, d_attended)
    heads_0 = Chain(*pair_0, scatter_bits)
    heads_0.step()
    back_1 = attend_backward(prob_1, mixed_1, after(d_context, heads_0.sent), 1)
    downs.step(back_1)
    ups.step(back_1)
    sums = jnp.concatenate(
        [
            jnp.concatenate([jnp.sum(back[0], axis=0, dtype=F32) for back in (back_0, back_1)])[None],
            jnp.concatenate([jnp.sum(back[2], axis=0, dtype=F32) for back in (back_0, back_1)])[None],
            sums_one[0:1],
            sums_two[0:1],
            sums_one[1:3],
            sums_two[1:3],
            up_bias.reshape(4, feature),
        ],
        axis=0,
    )
    sums = jnp.pad(sums.T.astype(BF), ((0, 0), (0, VEC_PAD - sums.shape[0])))
    pair_1 = qkv_grad(after(flipped, downs.sent, ups.sent), back_1, sums)
    downs.step(pair_1[0])
    ups.step(pair_1[0])
    heads_0.step(pair_1[0])
    heads_1 = Chain(after(pair_1[0], downs.sent, ups.sent, heads_0.sent), pair_1[1], scatter_bits)
    heads_1.step()
    input_grad = input_gradient(
        after(d_resid, downs.sent, ups.sent, heads_0.sent, heads_1.sent), (back_0, back_1), qkv_blocks
    )
    down_pieces = downs.finish()
    ups.step(input_grad)
    heads_0.step(input_grad)
    heads_1.step(input_grad)
    rates = step_rates()
    ordered = lambda *items: adam(*items, scatter_bits)
    g_down, n_down, f_down, s_down = ordered(
        [down_pieces], 0, feature, after(w_down, ups.sent, heads_0.sent, heads_1.sent), first_down, second_down, rates[3]
    )
    ups.step(g_down)
    heads_0.step(g_down)
    heads_1.step(g_down)
    up_pieces = ups.finish()
    sent = heads_0.sent, heads_1.sent
    g_up, n_up, f_up, s_up = ordered([up_pieces], 0, FF, after(w_up, *sent), first_up, second_up, rates[2])
    heads_0.step(g_up)
    heads_1.step(g_up)
    more = True
    while more:
        more = heads_0.step()
        more = heads_1.step() or more
    qkv_pieces = [heads_0.result, heads_1.result]
    g_out, n_out, f_out, s_out = ordered(
        [[piece[:, 3 * width :] for piece in qkv_pieces[0]]], 0, feature, w_out, first_out, second_out, rates[1]
    )
    g_qkv, n_qkv, f_qkv, s_qkv = ordered(qkv_pieces, 0, 3 * width, w_qkv, first_qkv, second_qkv, rates[0])
    vector_pieces = [piece[:, 3 * width : 3 * width + vectors.shape[0]] for piece in qkv_pieces[-1]]
    g_vec = in_order(vector_pieces, scatter_bits).T.astype(F32)
    n_vec, f_vec, s_vec = adam_update(vectors, g_vec, first_vectors, second_vectors, rates[4], 0.0)
    return (
        output.reshape(tokens.shape),
        input_grad.reshape(tokens.shape),
        g_qkv,
        g_out,
        g_up,
        g_down,
        g_vec,
        n_qkv,
        n_out,
        n_up,
        n_down,
        n_vec,
        f_qkv,
        f_out,
        f_up,
        f_down,
        f_vec,
        s_qkv,
        s_out,
        s_up,
        s_down,
        s_vec,
    )


def solution(mesh):
    placed = (
        P(("dp", "zero"), None, None),
        P(("dp", "zero"), None, None),
        P(("dp", "zero")),
        P("zero", None),
        P("zero", None),
        P("zero", None),
        P("zero", None),
        P(None, "zero"),
        P("zero", None),
        P("zero", None),
        P("zero", None),
        P("zero", None),
        P(None, "zero"),
        P("zero", None),
        P("zero", None),
        P("zero", None),
        P("zero", None),
        P(None, "zero"),
    )
    return jax.shard_map(
        body,
        mesh=mesh,
        in_specs=placed,
        out_specs=(
            P(("dp", "zero"), None, None),
            P(("dp", "zero"), None, None),
            P("zero", None),
            P("zero", None),
            P("zero", None),
            P("zero", None),
            P(None, "zero"),
            P("zero", None),
            P("zero", None),
            P("zero", None),
            P("zero", None),
            P(None, "zero"),
            P("zero", None),
            P("zero", None),
            P("zero", None),
            P("zero", None),
            P(None, "zero"),
            P("zero", None),
            P("zero", None),
            P("zero", None),
            P("zero", None),
            P(None, "zero"),
        ),
        check_vma=False,
    )
```
